512 devices in a mesh: lat: 16 (over x_hi, y, core), lon: 32 (over x_lo, z).
Axes of the slice: x: 4 (x_hi: 2, x_lo: 2; x = x_hi * 2 + x_lo), y: 4, z: 16, core: 2. Of those that a mesh axis runs over, the one named last changes fastest.
Arguments:
- adjoint_in: float32 [64, 256, 8192], P(None, 'lat', 'lon'), may hold values from -6 to 6
- u_courant: float32 [64, 256, 1024], P('lon', 'lat'), may hold values from -0.24 to 0.24
- v_courant: float32 [64, 256, 1024], P('lon', 'lat'), may hold values from -0.24 to 0.24
- diffusivity: float32 [64, 256, 1024], P('lon', 'lat'), may hold values from 0.025 to 1000
- surface_factor: float32 [256, 8192], P('lat', 'lon'), may hold values from 0.3 to 3
- zonal_sqrt: float32 [1024, 1024], P(None, 'lon'), may hold values from 0 to 1, as said below
Outputs:
- adjoint_out: float32 [64, 256, 8192], P(None, 'lat', 'lon')
- flux_gradient: float32 [256, 8192], P('lat', 'lon')
The draws below stay inside these ranges and needn't reach their ends.
Inputs may be any that keep to these rules, and one draw needn't show every extreme that they name: zonal_sqrt is symmetric and positive.
All inputs are finite; a program needn't handle non-finite values.
Results may differ from the reference program's by a relative error of at most 0.00013.
Values sent between devices are 32-bit elements; how exact they have to be, the bound alone decides.
A program may use at most 64 MiB of HBM per device.

```python
import math
import jax
import jax.numpy as jnp
from jax import lax

LEV = 64
TRAC = 8
NSUB = 4
NLAT = 256
NLON = 1024


def draw_zonal_sqrt(key, part):
    index_line = jnp.arange(NLON)
    distance = jnp.abs(index_line[:, None] - index_line[None, :])
    circle_gap = jnp.minimum(distance, NLON - distance).astype(jnp.float32)
    length = NLON / 8.0
    factors = jax.random.uniform(key, (NLON, NLON), jnp.float32, 0.5, 1.5)
    symmetric = 0.5 * (factors + factors.T)
    return jnp.exp(-circle_gap / length) * symmetric / jnp.sqrt(length)


def column_levels(key, low_log, high_log):
    column_key, level_key = jax.random.split(key)
    column_part = jnp.exp(jax.random.uniform(column_key, (1, NLAT, NLON), jnp.float32, low_log, high_log))
    level_part = jnp.exp(jax.random.uniform(level_key, (LEV, NLAT, NLON), jnp.float32, jnp.log(0.5), jnp.log(2.0)))
    return column_part * level_part


def draw_diffusivity(key, part):
    key = jax.random.fold_in(key, 11)
    return column_levels(key, jnp.log(0.05), jnp.log(200.0))


def level_of(stream_key, extent, cuts, least, high):
    loudness, own = 1.0, jax.random.fold_in(stream_key, 6)
    for axis_at, blocks in cuts:
        heights = jnp.exp(jax.random.uniform(jax.random.fold_in(own, axis_at), (blocks,), jnp.float32, least / len(cuts), high / len(cuts)))
        loudness = loudness * jnp.repeat(heights, extent[axis_at] // blocks).reshape([-1 if axis == axis_at else 1 for axis in range(len(extent))])
    return loudness


def bell_draw(stream_key, dims, scale, most, cuts=(), dtype=jnp.bfloat16):
    array = scale * jax.random.normal(stream_key, dims, jnp.float32)
    if cuts:
        array = array * level_of(stream_key, dims, cuts, -0.22, 0.18)
    return jnp.clip(array, -most, most).astype(dtype)


def setup_inputs(seed: int = 0) -> dict:
    key_list = jax.random.split(jax.random.key(seed), 7)
    return {
        "adjoint_in": bell_draw(key_list[0], (LEV, NLAT, NLON * TRAC), 1.0, 6.0, ((1, 16), (2, 32)), jnp.float32),
        "u_courant": jnp.clip(jax.random.uniform(key_list[1], (LEV, NLAT, NLON), jnp.float32, -0.24, 0.24) * level_of(key_list[1], (LEV, NLAT, NLON), ((0, 32), (1, 16)), -0.4, 0.0), -0.24, 0.24),
        "v_courant": jnp.clip(jax.random.uniform(key_list[2], (LEV, NLAT, NLON), jnp.float32, -0.24, 0.24) * level_of(key_list[2], (LEV, NLAT, NLON), ((0, 32), (1, 16)), -0.4, 0.0), -0.24, 0.24),
        "diffusivity": draw_diffusivity(jax.random.fold_in(key_list[6], 71), 0),
        "surface_factor": jnp.clip(jnp.exp(math.log(3.0) - 2.3025851 * jax.random.uniform(key_list[4], (NLAT, NLON * TRAC), jnp.float32) ** level_of(key_list[4], (NLAT, NLON * TRAC), ((0, 16), (1, 32)), -0.2, 0.2)), 0.3, 3.0),
        "zonal_sqrt": draw_zonal_sqrt(jax.random.fold_in(key_list[6], 71), 0),
    }


def transport(field, east, north):
    zero_row = jnp.zeros_like(field[:, :1])
    east_val = jnp.roll(field, -1, axis=2)
    west_val = jnp.roll(field, 1, axis=2)
    north_val = jnp.concatenate([field[:, 1:], zero_row], axis=1)
    south_val = jnp.concatenate([zero_row, field[:, :-1]], axis=1)
    west = jnp.roll(east, 1, axis=2)
    south = jnp.concatenate([jnp.zeros_like(north[:, :1]), north[:, :-1]], axis=1)
    result = field + jnp.maximum(east, 0.0) * (east_val - field)
    result = result + jnp.minimum(west, 0.0) * (field - west_val)
    result = result + jnp.maximum(north, 0.0) * (north_val - field)
    result = result + jnp.minimum(south, 0.0) * (field - south_val)
    return result

def vertical_solve(rhs, coef):
    below = jnp.concatenate([jnp.zeros_like(coef[:1]), coef[:-1]], axis=0)
    start = jnp.zeros_like(rhs[0])

    def forward(carry, slab):
        upper_c, upper_d = carry
        coef_k, below_k, rhs_k = slab
        denom = 1.0 + coef_k + below_k + below_k * upper_c
        new_c = -coef_k / denom
        new_d = (rhs_k + below_k * upper_d) / denom
        return ((new_c, new_d), (new_c, new_d))
    _, (c_all, d_all) = lax.scan(forward, (start, start), (coef, below, rhs))

    def backward(upper_x, slab):
        c_k, d_k = slab
        value = d_k - c_k * upper_x
        return (value, value)
    _, solved = lax.scan(backward, start, (c_all, d_all), reverse=True)
    return solved

def reference(adjoint_in, u_courant, v_courant, diffusivity, surface_factor, zonal_sqrt):
    field = adjoint_in.reshape(LEV, NLAT, NLON, TRAC)
    north_mask = (jnp.arange(NLAT) == NLAT - 1)[None, :, None]
    north_face = jnp.where(north_mask, 0.0, v_courant)
    east = u_courant[..., None]
    north = north_face[..., None]
    for substep in range(NSUB):
        field = transport(field, east, north)
    surface = surface_factor.reshape(NLAT, NLON, TRAC) * field[0]
    flux = jnp.einsum('imt,mj->ijt', surface, zonal_sqrt, precision=lax.Precision.HIGHEST)
    solved = vertical_solve(field, diffusivity[..., None])
    return (solved.reshape(LEV, NLAT, NLON * TRAC), flux.reshape(NLAT, NLON * TRAC))
```

```python
import jax
import jax.numpy as jnp
from jax import lax
from jax.experimental import pallas as pl
from jax.experimental.pallas import tpu as pltpu
from jax.sharding import PartitionSpec as P

MESH = pl.DeviceIdType.MESH
F32 = jnp.float32
NSUB = 4
TRAC = 8
NLA = 16
NLO = 32
NZ = 16
HALF = 8
CH = 4
PER = NLO // CH
LOOK = 3


def lon_of(slot):
    return lax.rem(slot, 2) * NZ + slot // 2


def slot_of(lon):
    return 2 * lax.rem(lon, NZ) + lon // NZ


def iota(axis):
    return lax.broadcasted_iota(jnp.int32, (8, 128), axis)


def lroll(value, shift):
    shift = shift % 128
    return value if shift == 0 else pltpu.roll(value, shift, 1)


def sroll(value, shift):
    shift = shift % 8
    return value if shift == 0 else pltpu.roll(value, shift, 0)


def lanes_of(value, index):
    return jnp.take_along_axis(value, index, axis=1, mode="promise_in_bounds")


def quarters(values, base):
    quarter = iota(1) // 32
    result = lroll(values[0], base)
    for q in range(1, 4):
        result = jnp.where(quarter == q, lroll(values[q], base + 32 * q), result)
    return result


def pack_slabs(u_v, v_v, k_v, uv_out, k_out, top):
    lane, sub = iota(1), iota(0)
    quarter, part = lane // 32, lax.rem(lane, 32) // 4

    def group(g, carry):
        def tile(ref, level, half, at):
            value = ref[level, 8 * half : 8 * half + 8, pl.ds(pl.multiple_of(at * 128, 128), 128)]
            if ref is v_v and half == 1:
                value = jnp.where(jnp.logical_and(top, sub == 7), 0.0, value)
            return value

        after, before = lax.rem(g + 1, 8), lax.rem(g + 7, 8)
        fields = [(u_v, 0), (u_v, 1), (v_v, 0), (v_v, 1)]
        edges = []
        for half in range(2):
            here = [tile(ref, level, half, g) for ref, level in fields]
            for w in range(4):
                slot = slot_of(4 * g + w)
                uv_out[slot, 16 * half : 16 * half + 8, :] = quarters(here, -32 * w)
            edge = jnp.zeros((8, 128), F32)
            for q, (ref, level) in enumerate(fields):
                west = jnp.where(lane >= 96, tile(ref, level, half, before), here[q])
                east = jnp.where(lane < 32, tile(ref, level, half, after), here[q])
                edge = jnp.where(part == 2 * q, lroll(west, 8 * q + 4), edge)
                edge = jnp.where(part == 2 * q + 1, lroll(east, 8 * q + 100), edge)
            edges.append(edge)
        kappa = [tile(k_v, level, half, g) for level in range(2) for half in range(2)]
        for w in range(4):
            slot = slot_of(4 * g + w)
            uv_out[slot, 8:16, :] = jnp.where(lane < 32, lroll(edges[0], -32 * w), lroll(edges[1], 32 - 32 * w))
            k_out[slot, :, :] = quarters(kappa, -32 * w)
        return carry

    lax.fori_loop(0, 8, group, 0)


def pack_halos(x_v, lon_out, lat_out):
    sub = iota(0)

    def one(slot, carry):
        lev = 2 * lon_of(slot)
        west, east = [], []
        for l in range(2):
            for half in range(2):
                west.append(x_v[lev + l, 8 * half : 8 * half + 8, 0:128])
                east.append(x_v[lev + l, 8 * half : 8 * half + 8, 128:256])
        lon_out[0, slot, :, :] = quarters(west, 0)
        lon_out[1, slot, :, :] = quarters(east, 32)
        for t, tiles in enumerate((west, east)):
            cols = slice(128 * t, 128 * t + 128)
            lat_out[0, slot, :, cols] = jnp.where(sub < 4, tiles[0], sroll(tiles[2], 4))
            lat_out[1, slot, :, cols] = jnp.where(sub >= 4, tiles[1], sroll(tiles[3], 4))
        return carry

    lax.fori_loop(0, NLO, one, 0)


def transport(slot, x_v, uv_in, uv_n, uv_s, lon_h, lon_n, lon_s, lat_n, lat_s):
    lane, sub = iota(1), iota(0)
    south_part = sub >= 4
    column = lane // 8
    rim = jnp.where(lane < 32, 4 + column, jnp.where(lane >= 96, column - 12, 0))
    lev = 2 * lon_of(slot)

    centre = [uv_in[slot, 0:8, :], uv_in[slot, 16:24, :], jnp.where(south_part, uv_s[slot, 8:16, :], uv_n[slot, 0:8, :])]
    edge_here = uv_in[slot, 8:16, :]
    edges = [edge_here, edge_here, jnp.where(south_part, lroll(uv_s[slot, 0:8, :], 96), uv_n[slot, 8:16, :])]
    edge_base = [0, 32, 0]

    def face(r, t, q):
        if t < 2:
            return lanes_of(centre[r], column + (16 * t + 32 * q))
        return lanes_of(edges[r], rim + (edge_base[r] + 8 * q))

    def lon_rim(east, west):
        return jnp.where(lane < 32, east, jnp.where(lane >= 96, west, 0.0))

    for l in range(2):
        lam = [[None] * 3 for _ in range(3)]
        for r in range(2):
            for t in range(2):
                lam[r][t] = x_v[lev + l, 8 * r : 8 * r + 8, 128 * t : 128 * t + 128]
            q = 2 * l + r
            lam[r][2] = lon_rim(lroll(lon_h[0, slot, :, :], -32 * q), lroll(lon_h[1, slot, :, :], 96 - 32 * q))
        for t in range(2):
            cols = slice(128 * t, 128 * t + 128)
            if l == 0:
                lam[2][t] = jnp.where(south_part, lat_s[slot, :, cols], lat_n[slot, :, cols])
            else:
                lam[2][t] = sroll(jnp.where(south_part, lat_n[slot, :, cols], lat_s[slot, :, cols]), 4)
        corner = []
        for side in range(2):
            base = 0 if side == 0 else 96
            corner.append(
                jnp.where(
                    south_part,
                    lroll(lon_s[side, slot, :, :], base - 32 * (2 * l + 1)),
                    lroll(lon_n[side, slot, :, :], base - 32 * (2 * l)),
                )
            )
        lam[2][2] = lon_rim(corner[0], corner[1])

        u = [[face(r, t, l) for t in range(3)] for r in range(3)]
        v = [[face(r, t, 2 + l) for t in range(3)] for r in range(3)]
        for step in range(NSUB):
            size = 3 if step < NSUB - 1 else 2
            keep = range(size)
            left = [[lroll(lam[r][t], -8) for t in range(3)] for r in range(3)]
            up = [[sroll(lam[r][t], -1) for t in range(3)] for r in range(3)]
            a = [[jnp.where(lane < 120, left[r][t], left[r][(t + 1) % 3]) - lam[r][t] for t in range(3)] for r in range(3)]
            b = [[jnp.where(sub < 7, up[r][t], up[(r + 1) % 3][t]) - lam[r][t] for t in range(3)] for r in range(3)]
            h = [[lroll(jnp.minimum(u[r][t], 0.0) * a[r][t], 8) for t in range(3)] for r in range(3)]
            w = [[sroll(jnp.minimum(v[r][t], 0.0) * b[r][t], 1) for t in range(3)] for r in range(3)]
            new = [[None] * 3 for _ in range(3)]
            for r in keep:
                for t in keep:
                    value = lam[r][t] + jnp.maximum(u[r][t], 0.0) * a[r][t]
                    value = value + jnp.where(lane >= 8, h[r][t], h[r][(t + 2) % 3])
                    value = value + jnp.maximum(v[r][t], 0.0) * b[r][t]
                    new[r][t] = value + jnp.where(sub >= 1, w[r][t], w[(r + 2) % 3][t])
            lam = new
        for r in range(2):
            for t in range(2):
                x_v[lev + l, 8 * r : 8 * r + 8, 128 * t : 128 * t + 128] = lam[r][t]


def factor(k_in, f_v, r_v):
    lane = iota(1)

    def one(m, p):
        both = k_in[slot_of(m), :, :]
        out = []
        for l in range(2):
            kappa = both if l == 0 else lroll(both, 64)
            inv = 1.0 / (p + kappa)
            frac = kappa * inv
            p = 1.0 + frac * p
            out.append((frac, inv))
        f_v[m, :, :] = jnp.where(lane < 64, out[0][0], lroll(out[1][0], 64))
        r_v[m, :, :] = jnp.where(lane < 64, out[0][1], lroll(out[1][1], 64))
        return p

    lax.fori_loop(0, NLO, one, jnp.ones((8, 128), F32))


def solve(x_v, f_v, r_v, start_out):
    column = iota(1) // 8
    places = [(h, t) for h in range(2) for t in range(2)]

    def spread(ref, m, l):
        tile = ref[m, :, :]
        return [lanes_of(tile, column + (64 * l + 32 * h + 16 * t)) for h, t in places]

    def at(level, h, t):
        return (level, slice(8 * h, 8 * h + 8), slice(128 * t, 128 * t + 128))

    def forward(m, carry):
        total, before = carry
        for l in range(2):
            total = [x_v[at(2 * m + l, h, t)] + f * s for (h, t), f, s in zip(places, before, total)]
            for (h, t), s in zip(places, total):
                x_v[at(2 * m + l, h, t)] = s
            before = spread(f_v, m, l)
        return (total, before)

    zeros = [jnp.zeros((8, 128), F32) for _ in places]
    lax.fori_loop(0, NLO, forward, (zeros, zeros))

    def backward(i, above):
        m = NLO - 1 - i
        for l in (1, 0):
            f, r = spread(f_v, m, l), spread(r_v, m, l)
            above = [r[n] * x_v[at(2 * m + l, *places[n])] + f[n] * above[n] for n in range(4)]
            for (h, t), s in zip(places, above):
                x_v[at(2 * m + l, h, t)] = s
        return above

    def chunk(c, above):
        above = lax.fori_loop(c * PER, c * PER + PER, backward, above)
        start_out(c)
        return above

    lax.fori_loop(0, CH, chunk, zeros)


def pack_surface(x_v, sf_v, turn, out):
    lane = lax.broadcasted_iota(jnp.int32, (32, 128), 1)
    for t in range(2):
        cols = slice(128 * t, 128 * t + 128)
        value = sf_v[:, cols] * x_v[0, :, cols]
        block = jnp.concatenate([value, jnp.zeros((112, 128), F32)], axis=0)
        turn[cols, :] = block.T
    total = turn[pl.ds(0, 32, stride=TRAC), :]
    for t in range(1, TRAC):
        piece = pltpu.roll(turn[pl.ds(t, 32, stride=TRAC), :], 16 * t, 1)
        total = jnp.where(jnp.logical_and(lane >= 16 * t, lane < 16 * t + 16), piece, total)
    out[...] = total


def unpack_flux(value, turn, out):
    for t in range(TRAC):
        piece = value if t == 0 else pltpu.roll(value, 128 - 16 * t, 1)
        turn[pl.ds(t, 32, stride=TRAC), :] = piece
    for t in range(2):
        cols = slice(128 * t, 128 * t + 128)
        out[:, cols] = turn[cols, :].T[:16]


def kernel(
    x_hbm, u_hbm, v_hbm, k_hbm, sf_hbm, z_hbm, out_hbm, flux_out,
    x_v, u_v, v_v, k_v, sf_v, z_v, zt_v,
    uv_out, uv_in, uv_n, uv_s, k_out, k_in, f_v, r_v,
    lon_out, lon_h, lon_n, lon_s, lat_out, lat_n, lat_s, turn, ring,
    in_sem, k_ss, k_rs, uv_ss, uv_rs, lat_ss, lat_rs, lon_ss, lon_rs,
    cor_ss, cor_rs, fwd_ss, fwd_rs, r_ss, l_ss, x_ss, ring_rs, out_sem, late_sem,
):
    a, me = lax.axis_index("lat"), lax.axis_index("lon")
    z, x = lax.rem(me, NZ), me // NZ
    mine = slot_of(me)
    early = z < HALF
    has_n, has_s = a < NLA - 1, a > 0
    east = x * NZ + z + 1
    east = lax.rem(me + 1, NLO)
    west = lax.rem(me + NLO - 1, NLO)

    loads = [
        pltpu.make_async_copy(src, dst, in_sem.at[i])
        for i, (src, dst) in enumerate(
            ((u_hbm, u_v), (v_hbm, v_v), (k_hbm, k_v), (x_hbm, x_v), (sf_hbm, sf_v), (z_hbm, z_v))
        )
    ]
    for load in loads:
        load.start()

    barrier = pltpu.get_barrier_semaphore()

    def greet(slot, carry):
        @pl.when(jnp.logical_and(slot != mine, jnp.logical_or(early, slot >= NLO // 2)))
        def _():
            pl.semaphore_signal(barrier, inc=1, device_id=(a, lon_of(slot)), device_id_type=MESH)

        return carry

    lax.fori_loop(0, NLO, greet, 0)

    @pl.when(has_n)
    def _():
        pl.semaphore_signal(barrier, inc=1, device_id=(a + 1, me), device_id_type=MESH)

    @pl.when(has_s)
    def _():
        pl.semaphore_signal(barrier, inc=1, device_id=(a - 1, me), device_id_type=MESH)

    for load in loads[:3]:
        load.wait()
    pack_slabs(u_v, v_v, k_v, uv_out, k_out, a == NLA - 1)
    loads[3].wait()
    pack_halos(x_v, lon_out, lat_out)

    uv_in[mine] = uv_out[mine]
    k_in[mine] = k_out[mine]

    @pl.when(jnp.logical_not(has_n))
    def _():
        lat_n[...] = jnp.zeros_like(lat_n)
        lon_n[...] = jnp.zeros_like(lon_n)
        uv_n[...] = jnp.zeros_like(uv_n)

    @pl.when(jnp.logical_not(has_s))
    def _():
        lat_s[...] = jnp.zeros_like(lat_s)
        lon_s[...] = jnp.zeros_like(lon_s)
        uv_s[...] = jnp.zeros_like(uv_s)

    neighbours = jnp.where(has_n, 1, 0) + jnp.where(has_s, 1, 0)

    pl.semaphore_wait(barrier, jnp.where(early, NLO // 2 - 1, NLO - 1) + neighbours)

    @pl.when(jnp.logical_not(early))
    def _():
        def greet_first(slot, carry):
            pl.semaphore_signal(late_sem, inc=1, device_id=(a, lon_of(slot)), device_id_type=MESH)
            return carry

        lax.fori_loop(0, NLO // 2, greet_first, 0)

    def remote(src, dst, ss, rs, device):
        return pltpu.make_async_remote_copy(
            src_ref=src, dst_ref=dst, send_sem=ss, recv_sem=rs, device_id=device, device_id_type=MESH
        )

    def span(c):
        return pl.ds(c * PER, PER)

    def send_k(slot):
        return remote(k_out.at[slot], k_in.at[mine], k_ss.at[slot], k_rs.at[mine], (a, lon_of(slot)))

    def send_uv(slot):
        return remote(uv_out.at[slot], uv_in.at[mine], uv_ss.at[slot], uv_rs.at[mine], (a, lon_of(slot)))

    def recv_k(slot):
        return remote(k_out.at[slot], k_in.at[slot], k_ss.at[slot], k_rs.at[slot], (a, lon_of(slot)))

    def recv_uv(slot):
        return remote(uv_out.at[slot], uv_in.at[slot], uv_ss.at[slot], uv_rs.at[slot], (a, lon_of(slot)))

    def lat_north(c):
        return remote(lat_out.at[1, span(c)], lat_s.at[span(c)], lat_ss.at[1, c], lat_rs.at[1, c], (a + 1, me))

    def lat_south(c):
        return remote(lat_out.at[0, span(c)], lat_n.at[span(c)], lat_ss.at[0, c], lat_rs.at[0, c], (a - 1, me))

    def lon_west(c):
        return remote(lon_out.at[0, span(c)], lon_h.at[0, span(c)], lon_ss.at[0, c], lon_rs.at[0, c], (a, west))

    def lon_east(c):
        return remote(lon_out.at[1, span(c)], lon_h.at[1, span(c)], lon_ss.at[1, c], lon_rs.at[1, c], (a, east))

    def cor_north(side, c):
        ref, dst = lon_h.at[side, span(c)], lon_s.at[side, span(c)]
        return remote(ref, dst, cor_ss.at[1, side, c], cor_rs.at[1, side, c], (a + 1, me))

    def cor_south(side, c):
        ref, dst = lon_h.at[side, span(c)], lon_n.at[side, span(c)]
        return remote(ref, dst, cor_ss.at[0, side, c], cor_rs.at[0, side, c], (a - 1, me))

    def fwd_north(slot):
        return remote(uv_in.at[slot, 8:24], uv_s.at[slot], fwd_ss.at[1, slot], fwd_rs.at[1, slot], (a + 1, me))

    def fwd_south(slot):
        return remote(uv_in.at[slot, 0:16], uv_n.at[slot], fwd_ss.at[0, slot], fwd_rs.at[0, slot], (a - 1, me))

    def each(count, action):
        def body(i, carry):
            action(i)
            return carry

        lax.fori_loop(0, count, body, 0)

    @pl.when(has_n)
    def _():
        each(CH, lambda c: lat_north(c).start())

    @pl.when(has_s)
    def _():
        each(CH, lambda c: lat_south(c).start())

    def spread_blocks(first, count):
        def one(i):
            slot = first + i

            @pl.when(slot != mine)
            def _():
                send_k(slot).start()
                send_uv(slot).start()

        each(count, one)

    far = HALF - 1
    east_first = jnp.where(early, z < far, z == NZ - 1)
    west_first = jnp.where(early, z > 0, z == HALF)

    @pl.when(east_first)
    def _():
        each(CH, lambda c: lon_east(c).start())

    @pl.when(west_first)
    def _():
        each(CH, lambda c: lon_west(c).start())

    spread_blocks(0, NLO // 2)

    @pl.when(early)
    def _():
        pl.semaphore_wait(late_sem, NLO // 2)

    @pl.when(jnp.logical_not(east_first))
    def _():
        each(CH, lambda c: lon_east(c).start())

    @pl.when(jnp.logical_not(west_first))
    def _():
        each(CH, lambda c: lon_west(c).start())

    spread_blocks(NLO // 2, NLO // 2)

    loads[4].wait()
    loads[5].wait()
    for i in range(8):
        zt_v[:, 128 * i : 128 * i + 128] = z_v[128 * i : 128 * i + 128, :].T

    def corners(c):
        lon_west(c).wait_recv()
        lon_east(c).wait_recv()

        @pl.when(has_n)
        def _():
            cor_north(0, c).start()
            cor_north(1, c).start()

        @pl.when(has_s)
        def _():
            cor_south(0, c).start()
            cor_south(1, c).start()

    each(CH, corners)

    def pass_on(slot):
        @pl.when(slot != mine)
        def _():
            recv_uv(slot).wait_recv()

        @pl.when(has_n)
        def _():
            fwd_north(slot).start()

        @pl.when(has_s)
        def _():
            fwd_south(slot).start()

    right = x * NZ + lax.rem(z + 1, NZ)
    left = x * NZ + lax.rem(z + NZ - 1, NZ)
    over = (1 - x) * NZ + z

    def ring_right(block, s):
        return remote(ring.at[block], ring.at[block], r_ss.at[s], ring_rs.at[block], (a, right))

    def ring_left(block, s):
        return remote(ring.at[block], ring.at[block], l_ss.at[s], ring_rs.at[block], (a, left))

    def ring_over(zz):
        block = x * NZ + zz
        return remote(ring.at[block], ring.at[block], x_ss.at[zz], ring_rs.at[block], (a, over))

    def ring_recv(block):
        return remote(ring.at[block], ring.at[block], x_ss.at[0], ring_rs.at[block], (a, over))

    def ring_start():
        pack_surface(x_v, sf_v, turn, ring.at[me])
        ring_right(me, 0).start()
        ring_left(me, 0).start()
        ring_over(z).start()

    def ring_step(s):
        zr = lax.rem(z - s + NZ, NZ)
        ring_recv(x * NZ + zr).wait_recv()

        @pl.when(s < NZ // 2)
        def _():
            ring_right(x * NZ + zr, s).start()

        ring_over(zr).start()

        @pl.when(s < NZ // 2)
        def _():
            zl = lax.rem(z + s, NZ)
            ring_recv(x * NZ + zl).wait_recv()

            @pl.when(s < NZ // 2 - 1)
            def _():
                ring_left(x * NZ + zl, s).start()

            ring_over(zl).start()

    each(LOOK, pass_on)

    def chunk(c):
        @pl.when(has_n)
        def _():
            lat_south(c).wait_recv()
            cor_south(0, c).wait_recv()
            cor_south(1, c).wait_recv()

        @pl.when(has_s)
        def _():
            lat_north(c).wait_recv()
            cor_north(0, c).wait_recv()
            cor_north(1, c).wait_recv()

        @pl.when(c == CH - 1)
        def _():
            def one(slot):
                @pl.when(slot != mine)
                def _():
                    recv_k(slot).wait_recv()

            each(NLO, one)
            factor(k_in, f_v, r_v)

        def one(j):
            slot = c * PER + j

            @pl.when(slot + LOOK < NLO)
            def _():
                pass_on(slot + LOOK)

            @pl.when(has_n)
            def _():
                fwd_south(slot).wait_recv()

            @pl.when(has_s)
            def _():
                fwd_north(slot).wait_recv()

            transport(slot, x_v, uv_in, uv_n, uv_s, lon_h, lon_n, lon_s, lat_n, lat_s)

            @pl.when(slot == 0)
            def _():
                ring_start()

            @pl.when(jnp.logical_and(slot >= NLO // 2, lax.rem(slot, 2) == 0))
            def _():
                ring_step((slot - NLO // 2) // 2 + 1)

        each(PER, one)

    each(CH, chunk)

    def store(c):
        levels = pl.ds((CH - 1 - c) * 2 * PER, 2 * PER)
        return pltpu.make_async_copy(x_v.at[levels], out_hbm.at[levels], out_sem.at[c])

    solve(x_v, f_v, r_v, lambda c: store(c).start())

    each(NZ, lambda zz: ring_recv((1 - x) * NZ + zz).wait_recv())
    gathered = ring[...].reshape(NLO * 32, 128)
    turned = jnp.dot(zt_v[...], gathered, precision=lax.Precision.HIGHEST, preferred_element_type=F32)
    unpack_flux(turned, turn, flux_out)

    def sent(slot):
        @pl.when(slot != mine)
        def _():
            send_k(slot).wait_send()
            send_uv(slot).wait_send()

        @pl.when(has_n)
        def _():
            fwd_north(slot).wait_send()

        @pl.when(has_s)
        def _():
            fwd_south(slot).wait_send()

    each(NLO, sent)

    def sent_chunk(c):
        lon_east(c).wait_send()
        lon_west(c).wait_send()

        @pl.when(has_n)
        def _():
            lat_north(c).wait_send()
            cor_north(0, c).wait_send()
            cor_north(1, c).wait_send()

        @pl.when(has_s)
        def _():
            lat_south(c).wait_send()
            cor_south(0, c).wait_send()
            cor_south(1, c).wait_send()

        store(c).wait()

    each(CH, sent_chunk)
    each(NZ // 2, lambda s: ring_right(me, s).wait_send())
    each(NZ // 2 - 1, lambda s: ring_left(me, s).wait_send())
    each(NZ, lambda zz: ring_over(zz).wait_send())


def on_device(adjoint_in, u_courant, v_courant, diffusivity, surface_factor, zonal_sqrt):
    def vmem(*shape):
        return pltpu.VMEM(shape, F32)

    def dma(*shape):
        return pltpu.SemaphoreType.DMA(shape)

    return pl.pallas_call(
        kernel,
        name="adjoint_hour",
        out_shape=(
            jax.ShapeDtypeStruct(adjoint_in.shape, F32),
            jax.ShapeDtypeStruct(surface_factor.shape, F32),
        ),
        in_specs=[pl.BlockSpec(memory_space=pl.ANY)] * 6,
        out_specs=(pl.BlockSpec(memory_space=pl.ANY), pl.BlockSpec(memory_space=pltpu.VMEM)),
        scratch_shapes=[
            vmem(64, 16, 256), vmem(2, 16, 1024), vmem(2, 16, 1024), vmem(2, 16, 1024),
            vmem(16, 256), vmem(1024, 32), vmem(32, 1024),
            vmem(32, 24, 128), vmem(32, 24, 128), vmem(32, 16, 128), vmem(32, 16, 128),
            vmem(32, 8, 128), vmem(32, 8, 128), vmem(32, 8, 128), vmem(32, 8, 128),
            vmem(2, 32, 8, 128), vmem(2, 32, 8, 128), vmem(2, 32, 8, 128), vmem(2, 32, 8, 128),
            vmem(2, 32, 8, 256), vmem(32, 8, 256), vmem(32, 8, 256), vmem(256, 128), vmem(32, 32, 128),
            dma(6), dma(32), dma(32), dma(32), dma(32), dma(2, CH), dma(2, CH), dma(2, CH), dma(2, CH),
            dma(2, 2, CH), dma(2, 2, CH), dma(2, 32), dma(2, 32), dma(8), dma(8), dma(16), dma(32), dma(CH),
            pltpu.SemaphoreType.REGULAR,
        ],
        compiler_params=pltpu.CompilerParams(
            collective_id=0, has_side_effects=True, vmem_limit_bytes=48 * 2**20
        ),
        cost_estimate=pl.CostEstimate(flops=60_000_000, bytes_accessed=3_000_000, transcendentals=0),
    )(adjoint_in, u_courant, v_courant, diffusivity, surface_factor, zonal_sqrt)


def solution(mesh):
    placed = (
        P(None, "lat", "lon"),
        P("lon", "lat", None),
        P("lon", "lat", None),
        P("lon", "lat", None),
        P("lat", "lon"),
        P(None, "lon"),
    )
    return jax.shard_map(
        on_device,
        mesh=mesh,
        in_specs=placed,
        out_specs=(P(None, "lat", "lon"), P("lat", "lon")),
        check_vma=False,
    )
```

```python
import jax
import jax.numpy as jnp
from jax import lax
from jax.experimental import pallas as pl
from jax.experimental.pallas import tpu as pltpu
from jax.sharding import PartitionSpec as P

MESH = pl.DeviceIdType.MESH
F32 = jnp.float32
NSUB = 4
TRAC = 8
NLA = 16
NLO = 32
NZ = 16
HALF = 8
LAG = 2
CH = 4
PER = 2
LOOK = 4
NG = 8


def lon_of(slot):
    group = slot // 4
    return lax.rem(group, 2) * NZ + (group // 2) * 4 + lax.rem(slot, 4)


def slot_of(lon):
    z = lax.rem(lon, NZ)
    return 8 * (z // 4) + 4 * (lon // NZ) + lax.rem(z, 4)


def iota(axis):
    return lax.broadcasted_iota(jnp.int32, (8, 128), axis)


def lroll(value, shift):
    shift = shift % 128
    return value if shift == 0 else pltpu.roll(value, shift, 1)


def sroll(value, shift):
    shift = shift % 8
    return value if shift == 0 else pltpu.roll(value, shift, 0)


def lanes_of(value, index):
    return jnp.take_along_axis(value, index, axis=1, mode="promise_in_bounds")


def quarters(values, base):
    quarter = iota(1) // 32
    result = lroll(values[0], base)
    for q in range(1, 4):
        result = jnp.where(quarter == q, lroll(values[q], base + 32 * q), result)
    return result


def rows16(slot):
    return pl.ds(pl.multiple_of(16 * slot, 16), 16)


def pack_slabs(u_v, v_v, k_v, uv_out, ek_out, top):
    lane, sub = iota(1), iota(0)
    part = lax.rem(lane, 32) // 4

    def group(g, carry):
        def tile(ref, level, half, at):
            value = ref[level, 8 * half : 8 * half + 8, pl.ds(pl.multiple_of(at * 128, 128), 128)]
            if ref is v_v and half == 1:
                value = jnp.where(jnp.logical_and(top, sub == 7), 0.0, value)
            return value

        after, before = lax.rem(g + 1, 8), lax.rem(g + 7, 8)
        rims = []
        for level in range(2):
            fields = [(u_v, 0), (v_v, 0), (u_v, 1), (v_v, 1)]
            here = [tile(ref, level, half, g) for ref, half in fields]
            for w in range(4):
                rows = pl.ds(pl.multiple_of(16 * slot_of(4 * g + w) + 8 * level, 8), 8)
                uv_out[rows, :] = quarters(here, -32 * w)
            rim = jnp.zeros((8, 128), F32)
            for q, (ref, half) in enumerate(fields):
                west = jnp.where(lane >= 96, tile(ref, level, half, before), here[q])
                east = jnp.where(lane < 32, tile(ref, level, half, after), here[q])
                rim = jnp.where(part == 2 * q, lroll(west, 8 * q + 4), rim)
                rim = jnp.where(part == 2 * q + 1, lroll(east, 8 * q + 100), rim)
            rims.append(rim)
        kappa = [tile(k_v, level, half, g) for level in range(2) for half in range(2)]
        for w in range(4):
            slot = slot_of(4 * g + w)
            both = jnp.where(lane < 32, lroll(rims[0], -32 * w), lroll(rims[1], 32 - 32 * w))
            both = jnp.where(lane < 64, both, lroll(sroll(both, 4), 64))
            ek_out[slot, 0, :, :] = both[0:4, :]
            block = quarters(kappa, -32 * w)
            ek_out[slot, 1, :, :] = block[0:4, :]
            ek_out[slot, 2, :, :] = block[4:8, :]
        return carry

    lax.fori_loop(0, 8, group, 0)


def level_base(group):
    return (lax.rem(group, 2) * 4 + group // 2) * 128


def level_rows(group, row):
    return pl.ds(level_base(group) + row, 8, stride=16)


def pack_halos(x_v, lon_out, lat_out):
    def one(group, carry):
        for b in range(4):
            west, east = [], []
            for i in range(4):
                west.append(x_v[0, level_rows(group, 4 * b + i), :])
                east.append(x_v[1, level_rows(group, 4 * b + i), :])
                if b in (0, 3):
                    side = 0 if b == 0 else 1
                    lat_out[side, group, i, :, 0:128] = west[i]
                    lat_out[side, group, i, :, 128:256] = east[i]
            lon_out[0, b, group, :, :] = quarters(west, 0)
            lon_out[1, b, group, :, :] = quarters(east, 32)
        return carry

    lax.fori_loop(0, NG, one, 0)


def transport(group, x_v, uv_in, uv_n, uv_s, e_in, e_n, e_s, lon_h, lon_n, lon_s, lat_n, lat_s, w, out, base):
    lane, sub = iota(1), iota(0)
    column = lane // 8
    rim = jnp.where(lane < 32, 4 + column, jnp.where(lane >= 96, column - 12, 0)) + 32 * lax.rem(sub, 2)

    parts = ((uv_in, e_in, 0, 0, 8, 4), (uv_in, e_in, 1, 0, 8, 12), (uv_n, e_n, 0, 0, 4, 20), (uv_s, e_s, 1, 4, 8, 0))

    def spread(f, carry):
        for half in range(2):
            for t in range(2):
                index = column + (64 * half + 16 * t + 32 * f)
                for uv, _, h, first, end, at in parts:
                    if h == half:
                        for r in range(first, end):
                            tile = uv[pl.ds(64 * group + r, 8, stride=8), :]
                            w[f, at + r - first, t, :, :] = lanes_of(tile, index)
            for j in range(2):
                index = rim + (64 * j + 16 * half + 8 * f)
                for _, e, h, first, end, at in parts:
                    if h == half:
                        for r in range(max(first, 4 * j), min(end, 4 * j + 4)):
                            edge = e[pl.ds(32 * group + r % 4, 8, stride=4), :]
                            w[f, at + r - first, 2, :, :] = lanes_of(edge, index)
        return carry

    lax.fori_loop(0, 2, spread, 0)

    def field(row):
        if row < 0:
            tiles = [lat_s[group, row + 4, :, 128 * t : 128 * t + 128] for t in range(2)]
            east, west = lon_s[0, group, :, :], lon_s[1, group, :, :]
        elif row >= 16:
            tiles = [lat_n[group, row - 16, :, 128 * t : 128 * t + 128] for t in range(2)]
            east, west = lon_n[0, group, :, :], lon_n[1, group, :, :]
        else:
            tiles = [x_v[t, level_rows(group, row), :] for t in range(2)]
            east, west = lon_h[0, row // 4, group, :, :], lon_h[1, row // 4, group, :, :]
        q = row % 4
        side = jnp.where(lane < 32, lroll(east, -32 * q), jnp.where(lane >= 96, lroll(west, 96 - 32 * q), 0.0))
        return tiles + [side]

    stages = [dict() for _ in range(NSUB + 1)]
    below = [None] * (NSUB + 1)
    for time in range(-4, 20 + LAG * NSUB):
        if time < 20:
            stages[0][time] = field(time)
        for step in range(NSUB, 0, -1):
            row = time - LAG * step
            before = stages[step - 1]
            if row not in before or row + 1 not in before:
                continue
            lower, upper = before.pop(row), before[row + 1]
            size = 3 if step < NSUB else 2
            v = [w[1, row + 4, t, :, :] for t in range(size)]
            b = [upper[t] - lower[t] for t in range(size)]
            south = below[step]
            below[step] = [jnp.minimum(v[t], 0.0) * b[t] for t in range(size)]
            if row == step - 5:
                continue
            u = [w[0, row + 4, t, :, :] for t in range(3)]
            left = [lroll(lower[t], -8) for t in range(3)]
            a = [jnp.where(lane < 120, left[t], left[(t + 1) % 3]) - lower[t] for t in range(3)]
            h = [lroll(jnp.minimum(u[t], 0.0) * a[t], 8) for t in range(3)]
            fresh = []
            for t in range(size):
                value = lower[t] + jnp.maximum(u[t], 0.0) * a[t]
                value = value + jnp.where(lane >= 8, h[t], h[(t + 2) % 3])
                value = value + jnp.maximum(v[t], 0.0) * b[t]
                fresh.append(value + south[t])
            if step < NSUB:
                stages[step][row] = fresh
            else:
                for t in range(2):
                    out[t, pl.ds(base + row, 8, stride=16), :] = fresh[t]


def factor(k_in, f_v, r_v):
    lane = iota(1)
    low = lane < 64

    def block(m):
        return k_in[pl.ds(pl.multiple_of(8 * slot_of(m), 8), 8), :]

    a = jnp.where(low, 1.0, 1.0 + block(31))
    b = jnp.ones((8, 128), F32)

    def four(i, carry):
        a, b = carry
        for n in range(4):
            m = 4 * i + n
            here, there = block(m), block(31 - m)
            beyond = block(jnp.maximum(30 - m, 0))
            for l in range(2):
                if l == 0:
                    kappa = jnp.where(low, here, lroll(there, 64))
                else:
                    kappa = jnp.where(low, lroll(here, 64), beyond)
                last = a * b
                nexta, nextb = a + kappa * (a + b), a + kappa * b
                inv = b / nextb
                f_v[2 * m + l, :, :] = kappa * inv
                r_v[2 * m + l, :, :] = inv
                if n == 3 and l == 1:
                    p = a / b
                    other = lroll(p, 64)
                    det = 1.0 / (p * other + kappa * (p + other))

                    @pl.when(i == 3)
                    def _():
                        f_v[31, :, :] = kappa * det
                        r_v[31, :, :] = (other + kappa) * det

                a, b = nexta, nextb
        scale = 1.0 / b
        return (a * scale, jnp.ones((8, 128), F32))

    lax.fori_loop(0, 4, four, (a, b))


PLACES = [(h, t) for h in range(2) for t in range(2)]


def widen(f_v, r_v, f_w, r_w):
    column = iota(1) // 8

    def some(i, carry):
        for end in range(2):
            for n, (h, t) in enumerate(PLACES):
                index = column + (64 * end + 32 * h + 16 * t)
                for src, dst in ((f_v, f_w), (r_v, r_w)):
                    for j in range(8):
                        dst[8 * i + j, 4 * end + n, :, :] = lanes_of(src[8 * i + j, :, :], index)
        return carry

    lax.fori_loop(0, 4, some, 0)


def solve(x_v, f_w, r_w, out):
    spots = [(end, h, t) for end in range(2) for h, t in PLACES]

    def rows(j, end, h):
        level = j if end == 0 else 63 - j
        return pl.ds(pl.multiple_of(16 * level + 8 * h, 8), 8)

    def forward(i, carry):
        total, before = carry
        for n in range(4):
            j = 4 * i + n
            total = [x_v[t, rows(j, end, h), :] + f * s for (end, h, t), f, s in zip(spots, before, total)]
            before = [f_w[j, n, :, :] for n in range(8)]
            for n, (end, h, t) in enumerate(spots):
                x_v[t, rows(j, end, h), :] = r_w[j, n, :, :] * total[n]
        return (total, before)

    zeros = [jnp.zeros((8, 128), F32) for _ in spots]
    total, before = lax.fori_loop(0, 8, forward, (zeros, zeros))
    above = [r_w[31, n, :, :] * total[n] + before[n] * total[(n + 4) % 8] for n in range(8)]

    def put(j, values):
        for n, (end, h, t) in enumerate(spots):
            out[rows(j, end, h), 128 * t : 128 * t + 128] = values[n]

    put(31, above)

    def one(j, above):
        above = [x_v[t, rows(j, end, h), :] + f_w[j, n, :, :] * above[n] for n, (end, h, t) in enumerate(spots)]
        put(j, above)
        return above

    for n in range(1, 8):
        above = one(31 - n, above)

    def chunk(c, above):
        for n in range(8):
            above = one(31 - 8 * c - n, above)
        return above

    lax.fori_loop(1, 4, chunk, above)


def pack_surface(x_v, sf_v, turn, out):
    lane = lax.broadcasted_iota(jnp.int32, (32, 128), 1)
    for t in range(2):
        cols = slice(128 * t, 128 * t + 128)
        value = sf_v[:, cols] * x_v[t, 0:16, :]
        block = jnp.concatenate([value, jnp.zeros((112, 128), F32)], axis=0)
        turn[cols, :] = block.T
    total = turn[pl.ds(0, 32, stride=TRAC), :]
    for t in range(1, TRAC):
        piece = pltpu.roll(turn[pl.ds(t, 32, stride=TRAC), :], 16 * t, 1)
        total = jnp.where(jnp.logical_and(lane >= 16 * t, lane < 16 * t + 16), piece, total)
    out[...] = total


def unpack_flux(value, turn, out):
    for t in range(TRAC):
        piece = value if t == 0 else pltpu.roll(value, 128 - 16 * t, 1)
        turn[pl.ds(t, 32, stride=TRAC), :] = piece
    for t in range(2):
        cols = slice(128 * t, 128 * t + 128)
        out[:, cols] = turn[cols, :].T[:16]


def kernel(
    x_hbm, u_hbm, v_hbm, k_hbm, sf_hbm, zt_hbm, out, flux_out,
    x_v, u_v, v_v, k_v, sf_v, zt_v,
    uv_out, uv_in, uv_n, uv_s, ek_out, ek_in, e_in, e_n, e_s, k_in, f_v, r_v, f_w, r_w, w_v,
    lon_out, lon_h, lon_n, lon_s, lat_out, lat_n, lat_s, turn, ring, out_v,
    uv0_in, uv0_n, uv0_s, e0_in, e0_n, e0_s, y_v,
    in_sem, ek_ss, ek_rs, uv_ss, uv_rs, lat_ss, lat_rs, lon_ss, lon_rs,
    cor_ss, cor_rs, fwd_ss, fwd_rs, far_ss, near_ss, x_ss, ring_rs, out_sem, first_ss, first_rs,
):
    a, me = lax.axis_index("lat"), lax.axis_index("lon")
    z, x = lax.rem(me, NZ), me // NZ
    mine = slot_of(me)
    early = z < HALF
    has_n, has_s = a < NLA - 1, a > 0
    east = lax.rem(me + 1, NLO)
    west = lax.rem(me + NLO - 1, NLO)

    def tiled(ref, t):
        return ref.at[:, 128 * t : 128 * t + 128]

    pairs = ((u_hbm, u_v), (v_hbm, v_v), (k_hbm, k_v), (tiled(x_hbm, 0), x_v.at[0]), (tiled(x_hbm, 1), x_v.at[1]), (sf_hbm, sf_v), (zt_hbm, zt_v))
    loads = [pltpu.make_async_copy(src, dst, in_sem.at[i]) for i, (src, dst) in enumerate(pairs)]
    for load in loads:
        load.start()

    def each(count, action):
        def body(i, carry):
            action(i)
            return carry

        lax.fori_loop(0, count, body, 0)

    barrier = pltpu.get_barrier_semaphore()

    def nth(j):
        return lax.rem(j, 2) * NZ + j // 2

    def greet(lon):
        @pl.when(lon != me)
        def _():
            pl.semaphore_signal(barrier, inc=1, device_id=(a, lon), device_id_type=MESH)

    each(NLO // 2, lambda j: greet(nth(NLO // 2 + j)))

    each(NLO // 2, lambda j: greet(nth(j)))

    @pl.when(has_n)
    def _():
        pl.semaphore_signal(barrier, inc=1, device_id=(a + 1, me), device_id_type=MESH)

    @pl.when(has_s)
    def _():
        pl.semaphore_signal(barrier, inc=1, device_id=(a - 1, me), device_id_type=MESH)

    for load in loads[:3]:
        load.wait()
    pack_slabs(u_v, v_v, k_v, uv_out, ek_out, a == NLA - 1)
    loads[3].wait()
    loads[4].wait()
    pack_halos(x_v, lon_out, lat_out)

    uv_in[rows16(mine), :] = uv_out[rows16(mine), :]
    ek_in[mine] = ek_out[mine]

    @pl.when(jnp.logical_not(has_n))
    def _():
        for ref in (lat_n, lon_n, uv_n, e_n, uv0_n, e0_n):
            ref[...] = jnp.zeros_like(ref)

    @pl.when(jnp.logical_not(has_s))
    def _():
        for ref in (lat_s, lon_s, uv_s, e_s, uv0_s, e0_s):
            ref[...] = jnp.zeros_like(ref)

    for ref in (uv0_in, uv0_n, uv0_s):
        ref[16:64, :] = jnp.zeros((48, 128), F32)
    for ref in (e0_in, e0_n, e0_s):
        ref[8:32, :] = jnp.zeros((24, 128), F32)

    neighbours = jnp.where(has_n, 1, 0) + jnp.where(has_s, 1, 0)
    pl.semaphore_wait(barrier, NLO - 1 + neighbours)

    def remote(src, dst, ss, rs, device):
        return pltpu.make_async_remote_copy(
            src_ref=src, dst_ref=dst, send_sem=ss, recv_sem=rs, device_id=device, device_id_type=MESH
        )

    def send_ek(lon):
        s = slot_of(lon)
        return remote(ek_out.at[s], ek_in.at[mine], ek_ss.at[s], ek_rs.at[mine], (a, lon))

    def send_uv(lon):
        s = slot_of(lon)
        return remote(uv_out.at[rows16(s)], uv_in.at[rows16(mine)], uv_ss.at[s], uv_rs.at[mine], (a, lon))

    def recv_ek(slot):
        return remote(ek_out.at[slot], ek_in.at[slot], ek_ss.at[slot], ek_rs.at[slot], (a, lon_of(slot)))

    def recv_uv(slot):
        rows = rows16(slot)
        return remote(uv_out.at[rows], uv_in.at[rows], uv_ss.at[slot], uv_rs.at[slot], (a, lon_of(slot)))

    def span(c):
        return pl.ds(c * PER, PER)

    def lat_north(c):
        return remote(lat_out.at[1, span(c)], lat_s.at[span(c)], lat_ss.at[1, c], lat_rs.at[1, c], (a + 1, me))

    def lat_south(c):
        return remote(lat_out.at[0, span(c)], lat_n.at[span(c)], lat_ss.at[0, c], lat_rs.at[0, c], (a - 1, me))

    def lon_west(c):
        return remote(lon_out.at[0, :, span(c)], lon_h.at[0, :, span(c)], lon_ss.at[0, c], lon_rs.at[0, c], (a, west))

    def lon_east(c):
        return remote(lon_out.at[1, :, span(c)], lon_h.at[1, :, span(c)], lon_ss.at[1, c], lon_rs.at[1, c], (a, east))

    def cor_north(side, c):
        ref, dst = lon_h.at[side, 3, span(c)], lon_s.at[side, span(c)]
        return remote(ref, dst, cor_ss.at[1, side, c], cor_rs.at[1, side, c], (a + 1, me))

    def cor_south(side, c):
        ref, dst = lon_h.at[side, 0, span(c)], lon_n.at[side, span(c)]
        return remote(ref, dst, cor_ss.at[0, side, c], cor_rs.at[0, side, c], (a - 1, me))

    def uv_rows(group):
        return pl.ds(pl.multiple_of(64 * group, 64), 64)

    def e_rows(group):
        return pl.ds(pl.multiple_of(32 * group, 32), 32)

    def fwd_north(group):
        r, e = uv_rows(group), e_rows(group)
        return (
            remote(uv_in.at[r], uv_s.at[r], fwd_ss.at[1, 0, group], fwd_rs.at[1, 0, group], (a + 1, me)),
            remote(e_in.at[e], e_s.at[e], fwd_ss.at[1, 1, group], fwd_rs.at[1, 1, group], (a + 1, me)),
        )

    def fwd_south(group):
        r, e = uv_rows(group), e_rows(group)
        return (
            remote(uv_in.at[r], uv_n.at[r], fwd_ss.at[0, 0, group], fwd_rs.at[0, 0, group], (a - 1, me)),
            remote(e_in.at[e], e_n.at[e], fwd_ss.at[0, 1, group], fwd_rs.at[0, 1, group], (a - 1, me)),
        )

    def spread_blocks(order, first, count):
        def one(i):
            lon = lax.rem(first + i, 2) * NZ + order(first + i)

            @pl.when(lon != me)
            def _():
                send_ek(lon).start()
                send_uv(lon).start()

        each(count, one)

    def send_halos(first, count):
        def one(i):
            lon_east(first + i).start()
            lon_west(first + i).start()

            @pl.when(has_n)
            def _():
                lat_north(first + i).start()

            @pl.when(has_s)
            def _():
                lat_south(first + i).start()

        each(count, one)

    def place_at(j):
        return jnp.where(me == 0, NZ - 1 - j // 2, j // 2)

    send_halos(0, 1)
    spread_blocks(place_at, 0, NLO // 4)
    send_halos(1, CH - 1)
    spread_blocks(place_at, NLO // 4, NLO - NLO // 4)

    loads[5].wait()
    loads[6].wait()

    def corners(c):
        lon_west(c).wait_recv()
        lon_east(c).wait_recv()

        @pl.when(has_n)
        def _():
            cor_north(0, c).start()
            cor_north(1, c).start()

        @pl.when(has_s)
        def _():
            cor_south(0, c).start()
            cor_south(1, c).start()

    def halos_here(c):
        @pl.when(has_n)
        def _():
            lat_south(c).wait_recv()
            cor_south(0, c).wait_recv()
            cor_south(1, c).wait_recv()

        @pl.when(has_s)
        def _():
            lat_north(c).wait_recv()
            cor_north(0, c).wait_recv()
            cor_north(1, c).wait_recv()

    def first_north():
        return (
            remote(uv0_in.at[0:16], uv0_s.at[0:16], first_ss.at[1, 0], first_rs.at[1, 0], (a + 1, me)),
            remote(e0_in.at[0:8], e0_s.at[0:8], first_ss.at[1, 1], first_rs.at[1, 1], (a + 1, me)),
        )

    def first_south():
        return (
            remote(uv0_in.at[0:16], uv0_n.at[0:16], first_ss.at[0, 0], first_rs.at[0, 0], (a - 1, me)),
            remote(e0_in.at[0:8], e0_n.at[0:8], first_ss.at[0, 1], first_rs.at[0, 1], (a - 1, me)),
        )

    corners(0)

    @pl.when(me != 0)
    def _():
        recv_ek(0).wait_recv()
        recv_uv(0).wait_recv()

    uv0_in[0:16, :] = uv_in[0:16, :]
    e0_in[0:8, :] = jnp.concatenate([ek_in[0, 0, :, :], ek_in[0, 0, :, :]], axis=0)

    @pl.when(has_n)
    def _():
        for copy in first_north():
            copy.start()

    @pl.when(has_s)
    def _():
        for copy in first_south():
            copy.start()

    each(CH - 1, lambda c: corners(c + 1))

    def pass_on(group):
        def one(i):
            slot = 4 * group + i

            @pl.when(jnp.logical_and(slot != mine, slot != 0))
            def _():
                recv_ek(slot).wait_recv()
                recv_uv(slot).wait_recv()

            rims = ek_in[slot, 0, :, :]
            at = pl.multiple_of(8 * slot, 8)
            e_in[pl.ds(at, 8), :] = jnp.concatenate([rims, rims], axis=0)
            k_in[pl.ds(at, 8), :] = jnp.concatenate([ek_in[slot, 1, :, :], ek_in[slot, 2, :, :]], axis=0)

        each(4, one)

        @pl.when(has_n)
        def _():
            for copy in fwd_north(group):
                copy.start()

        @pl.when(has_s)
        def _():
            for copy in fwd_south(group):
                copy.start()

    over = (1 - x) * NZ + z

    def place(d):
        return lax.rem(z + d, NZ)

    FAR, NEAR = (4, 12, 8), (1, 15, 2)

    def ring_send(block, device, sem):
        return remote(ring.at[block], ring.at[block], sem, ring_rs.at[block], (a, device))

    def ring_far(i):
        return ring_send(me, x * NZ + place(FAR[i]), far_ss.at[i])

    def ring_near(k, i):
        block = x * NZ + place((0, 4, 12, 8)[k])
        return ring_send(block, x * NZ + place(NEAR[i]), near_ss.at[k, i])

    def ring_over(d):
        zz = place(d)
        return ring_send(x * NZ + zz, over, x_ss.at[zz])

    def ring_recv(block):
        return ring_send(block, over, x_ss.at[0])

    def ring_start():
        pack_surface(y_v, sf_v, turn, ring.at[me])
        for i in range(3):
            ring_far(i).start()
        ring_over(0).start()
        for i in range(3):
            ring_near(0, i).start()

    def ring_middle():
        for k, d in enumerate((4, 12, 8)):
            ring_recv(x * NZ + place(d)).wait_recv()
            for i in range(3):
                ring_near(k + 1, i).start()
            ring_over(d).start()

    def ring_end():
        for d in range(NZ):
            if d % 4:
                ring_recv(x * NZ + place(d)).wait_recv()
                ring_over(d).start()

    halos_here(0)

    @pl.when(has_n)
    def _():
        for copy in first_south():
            copy.wait_recv()

    @pl.when(has_s)
    def _():
        for copy in first_north():
            copy.wait_recv()

    transport(0, x_v, uv0_in, uv0_n, uv0_s, e0_in, e0_n, e0_s, lon_h, lon_n, lon_s, lat_n, lat_s, w_v, y_v, 0)
    ring_start()
    ring_middle()
    each(LOOK, pass_on)

    def turn_of(group):
        @pl.when(group + LOOK < NG)
        def _():
            pass_on(group + LOOK)

        @pl.when(jnp.logical_and(lax.rem(group, PER) == 0, group > 0))
        def _():
            halos_here(group // PER)

        @pl.when(has_n)
        def _():
            for copy in fwd_south(group):
                copy.wait_recv()

        @pl.when(has_s)
        def _():
            for copy in fwd_north(group):
                copy.wait_recv()

        transport(
            group, x_v, uv_in, uv_n, uv_s, e_in, e_n, e_s, lon_h, lon_n, lon_s, lat_n, lat_s, w_v, x_v, level_base(group)
        )

        @pl.when(group == 1)
        def _():
            ring_end()

        @pl.when(group == NG - 2)
        def _():
            factor(k_in, f_v, r_v)
            widen(f_v, r_v, f_w, r_w)

    each(NG, turn_of)

    def store(c):
        rows = pl.ds(256 * c, 256)
        return pltpu.make_async_copy(out_v.at[rows], out.at[rows], out_sem.at[c])

    solve(x_v, f_w, r_w, out_v)
    for c in range(4):
        store(c).start()

    each(NZ, lambda zz: ring_recv((1 - x) * NZ + zz).wait_recv())
    gathered = ring[...].reshape(NLO * 32, 128)
    turned = jnp.dot(zt_v[...], gathered, precision=lax.Precision.HIGHEST, preferred_element_type=F32)
    unpack_flux(turned, turn, flux_out)

    def sent(lon):
        @pl.when(lon != me)
        def _():
            send_ek(lon).wait_send()
            send_uv(lon).wait_send()

    each(NLO, sent)
    for c in range(4):
        store(c).wait()

    def sent_group(group):
        @pl.when(has_n)
        def _():
            for copy in fwd_north(group):
                copy.wait_send()

        @pl.when(has_s)
        def _():
            for copy in fwd_south(group):
                copy.wait_send()

    each(NG, sent_group)

    @pl.when(has_n)
    def _():
        for copy in first_north():
            copy.wait_send()

    @pl.when(has_s)
    def _():
        for copy in first_south():
            copy.wait_send()

    def sent_chunk(c):
        lon_east(c).wait_send()
        lon_west(c).wait_send()

        @pl.when(has_n)
        def _():
            lat_north(c).wait_send()
            cor_north(0, c).wait_send()
            cor_north(1, c).wait_send()

        @pl.when(has_s)
        def _():
            lat_south(c).wait_send()
            cor_south(0, c).wait_send()
            cor_south(1, c).wait_send()

    each(CH, sent_chunk)
    for i in range(3):
        ring_far(i).wait_send()
        for k in range(4):
            ring_near(k, i).wait_send()
    each(NZ, lambda d: ring_over(d).wait_send())


def on_device(adjoint_in, u_courant, v_courant, diffusivity, surface_factor, zonal_sqrt):
    def vmem(*shape):
        return pltpu.VMEM(shape, F32)

    def dma(*shape):
        return pltpu.SemaphoreType.DMA(shape)

    solved, flux = pl.pallas_call(
        kernel,
        name="adjoint_hour",
        out_shape=(
            jax.ShapeDtypeStruct((1024, 256), F32),
            jax.ShapeDtypeStruct(surface_factor.shape, F32),
        ),
        in_specs=[pl.BlockSpec(memory_space=pltpu.HBM)] * 6,
        out_specs=(pl.BlockSpec(memory_space=pl.ANY), pl.BlockSpec(memory_space=pltpu.VMEM)),
        scratch_shapes=[
            vmem(2, 1024, 128), vmem(2, 16, 1024), vmem(2, 16, 1024), vmem(2, 16, 1024),
            vmem(16, 256), vmem(32, 1024),
            vmem(512, 128), vmem(512, 128), vmem(512, 128), vmem(512, 128),
            vmem(32, 3, 4, 128), vmem(32, 3, 4, 128), vmem(256, 128), vmem(256, 128), vmem(256, 128), vmem(256, 128),
            vmem(32, 8, 128), vmem(32, 8, 128), vmem(32, 8, 8, 128), vmem(32, 8, 8, 128), vmem(2, 24, 3, 8, 128),
            vmem(2, 4, 8, 8, 128), vmem(2, 4, 8, 8, 128), vmem(2, 8, 8, 128), vmem(2, 8, 8, 128),
            vmem(2, 8, 4, 8, 256), vmem(8, 4, 8, 256), vmem(8, 4, 8, 256), vmem(256, 128), vmem(32, 32, 128), vmem(1024, 256),
            vmem(64, 128), vmem(64, 128), vmem(64, 128), vmem(32, 128), vmem(32, 128), vmem(32, 128), vmem(2, 128, 128),
            dma(7), dma(32), dma(32), dma(32), dma(32), dma(2, CH), dma(2, CH), dma(2, CH), dma(2, CH),
            dma(2, 2, CH), dma(2, 2, CH), dma(2, 2, NG), dma(2, 2, NG), dma(3), dma(4, 3), dma(16), dma(32), dma(4), dma(2, 2), dma(2, 2),
        ],
        compiler_params=pltpu.CompilerParams(
            collective_id=0, has_side_effects=True, vmem_limit_bytes=56 * 2**20
        ),
        cost_estimate=pl.CostEstimate(flops=60_000_000, bytes_accessed=3_000_000, transcendentals=0),
    )(adjoint_in.reshape(1024, 256), u_courant, v_courant, diffusivity, surface_factor, zonal_sqrt.T)
    return solved.reshape(adjoint_in.shape), flux


def solution(mesh):
    placed = (
        P(None, "lat", "lon"),
        P("lon", "lat", None),
        P("lon", "lat", None),
        P("lon", "lat", None),
        P("lat", "lon"),
        P(None, "lon"),
    )
    return jax.shard_map(
        on_device,
        mesh=mesh,
        in_specs=placed,
        out_specs=(P(None, "lat", "lon"), P("lat", "lon")),
        check_vma=False,
    )
```

```python
import jax
import jax.numpy as jnp
from jax import lax
from jax.experimental import pallas as pl
from jax.experimental.pallas import tpu as pltpu
from jax.sharding import PartitionSpec as P

MESH = pl.DeviceIdType.MESH
F32 = jnp.float32
NSUB = 4
TRAC = 8
NLA = 16
NLO = 32
NZ = 16
HALF = 8
LAG = 2
CH = 4
PER = 2
LOOK = 4
NG = 8


def lon_of(slot):
    group = slot // 4
    return lax.rem(group, 2) * NZ + (group // 2) * 4 + lax.rem(slot, 4)


def slot_of(lon):
    z = lax.rem(lon, NZ)
    return 8 * (z // 4) + 4 * (lon // NZ) + lax.rem(z, 4)


def iota(axis):
    return lax.broadcasted_iota(jnp.int32, (8, 128), axis)


def lroll(value, shift):
    shift = shift % 128
    return value if shift == 0 else pltpu.roll(value, shift, 1)


def sroll(value, shift):
    shift = shift % 8
    return value if shift == 0 else pltpu.roll(value, shift, 0)


def lanes_of(value, index):
    return jnp.take_along_axis(value, index, axis=1, mode="promise_in_bounds")


def quarters(values, base):
    quarter = iota(1) // 32
    result = lroll(values[0], base)
    for q in range(1, 4):
        result = jnp.where(quarter == q, lroll(values[q], base + 32 * q), result)
    return result


def rows16(slot):
    return pl.ds(pl.multiple_of(16 * slot, 16), 16)


def pack_slabs(u_v, v_v, k_v, uv_out, ek_out, top):
    lane, sub = iota(1), iota(0)
    part = lax.rem(lane, 32) // 4

    def group(g, carry):
        def tile(ref, level, half, at):
            value = ref[level, 8 * half : 8 * half + 8, pl.ds(pl.multiple_of(at * 128, 128), 128)]
            if ref is v_v and half == 1:
                value = jnp.where(jnp.logical_and(top, sub == 7), 0.0, value)
            return value

        after, before = lax.rem(g + 1, 8), lax.rem(g + 7, 8)
        rims = []
        for level in range(2):
            fields = [(u_v, 0), (v_v, 0), (u_v, 1), (v_v, 1)]
            here = [tile(ref, level, half, g) for ref, half in fields]
            for w in range(4):
                rows = pl.ds(pl.multiple_of(16 * slot_of(4 * g + w) + 8 * level, 8), 8)
                uv_out[rows, :] = quarters(here, -32 * w)
            rim = jnp.zeros((8, 128), F32)
            for q, (ref, half) in enumerate(fields):
                west = jnp.where(lane >= 96, tile(ref, level, half, before), here[q])
                east = jnp.where(lane < 32, tile(ref, level, half, after), here[q])
                rim = jnp.where(part == 2 * q, lroll(west, 8 * q + 4), rim)
                rim = jnp.where(part == 2 * q + 1, lroll(east, 8 * q + 100), rim)
            rims.append(rim)
        kappa = [tile(k_v, level, half, g) for level in range(2) for half in range(2)]
        for w in range(4):
            slot = slot_of(4 * g + w)
            both = jnp.where(lane < 32, lroll(rims[0], -32 * w), lroll(rims[1], 32 - 32 * w))
            both = jnp.where(lane < 64, both, lroll(sroll(both, 4), 64))
            ek_out[slot, 0, :, :] = both[0:4, :]
            block = quarters(kappa, -32 * w)
            ek_out[slot, 1, :, :] = block[0:4, :]
            ek_out[slot, 2, :, :] = block[4:8, :]
        return carry

    lax.fori_loop(0, 8, group, 0)


def level_base(group):
    return (lax.rem(group, 2) * 4 + group // 2) * 128


def level_rows(group, row):
    return pl.ds(level_base(group) + row, 8, stride=16)


def pack_halos(x_v, lon_out, lat_out):
    def one(group, carry):
        for b in range(4):
            west, east = [], []
            for i in range(4):
                west.append(x_v[0, level_rows(group, 4 * b + i), :])
                east.append(x_v[1, level_rows(group, 4 * b + i), :])
                if b in (0, 3):
                    side = 0 if b == 0 else 1
                    lat_out[side, group, i, :, 0:128] = west[i]
                    lat_out[side, group, i, :, 128:256] = east[i]
            lon_out[0, b, group, :, :] = quarters(west, 0)
            lon_out[1, b, group, :, :] = quarters(east, 32)
        return carry

    lax.fori_loop(0, NG, one, 0)


def transport(group, x_v, uv_in, uv_n, uv_s, e_in, e_n, e_s, lon_h, lon_n, lon_s, lat_n, lat_s, w, out, base):
    lane, sub = iota(1), iota(0)
    column = lane // 8
    rim = jnp.where(lane < 32, 4 + column, jnp.where(lane >= 96, column - 12, 0)) + 32 * lax.rem(sub, 2)

    parts = ((uv_in, e_in, 0, 0, 8, 4), (uv_in, e_in, 1, 0, 8, 12), (uv_n, e_n, 0, 0, 4, 20), (uv_s, e_s, 1, 4, 8, 0))

    def spread(f, carry):
        for half in range(2):
            for t in range(2):
                index = column + (64 * half + 16 * t + 32 * f)
                for uv, _, h, first, end, at in parts:
                    if h == half:
                        for r in range(first, end):
                            tile = uv[pl.ds(64 * group + r, 8, stride=8), :]
                            w[f, at + r - first, t, :, :] = lanes_of(tile, index)
            for j in range(2):
                index = rim + (64 * j + 16 * half + 8 * f)
                for _, e, h, first, end, at in parts:
                    if h == half:
                        for r in range(max(first, 4 * j), min(end, 4 * j + 4)):
                            edge = e[pl.ds(32 * group + r % 4, 8, stride=4), :]
                            w[f, at + r - first, 2, :, :] = lanes_of(edge, index)
        return carry

    lax.fori_loop(0, 2, spread, 0)

    def field(row):
        if row < 0:
            tiles = [lat_s[group, row + 4, :, 128 * t : 128 * t + 128] for t in range(2)]
            east, west = lon_s[0, group, :, :], lon_s[1, group, :, :]
        elif row >= 16:
            tiles = [lat_n[group, row - 16, :, 128 * t : 128 * t + 128] for t in range(2)]
            east, west = lon_n[0, group, :, :], lon_n[1, group, :, :]
        else:
            tiles = [x_v[t, level_rows(group, row), :] for t in range(2)]
            east, west = lon_h[0, row // 4, group, :, :], lon_h[1, row // 4, group, :, :]
        q = row % 4
        side = jnp.where(lane < 32, lroll(east, -32 * q), jnp.where(lane >= 96, lroll(west, 96 - 32 * q), 0.0))
        return tiles + [side]

    stages = [dict() for _ in range(NSUB + 1)]
    below = [None] * (NSUB + 1)
    for time in range(-4, 20 + LAG * NSUB):
        if time < 20:
            stages[0][time] = field(time)
        for step in range(NSUB, 0, -1):
            row = time - LAG * step
            before = stages[step - 1]
            if row not in before or row + 1 not in before:
                continue
            lower, upper = before.pop(row), before[row + 1]
            size = 3 if step < NSUB else 2
            v = [w[1, row + 4, t, :, :] for t in range(size)]
            b = [upper[t] - lower[t] for t in range(size)]
            south = below[step]
            below[step] = [jnp.minimum(v[t], 0.0) * b[t] for t in range(size)]
            if row == step - 5:
                continue
            u = [w[0, row + 4, t, :, :] for t in range(3)]
            left = [lroll(lower[t], -8) for t in range(3)]
            a = [jnp.where(lane < 120, left[t], left[(t + 1) % 3]) - lower[t] for t in range(3)]
            h = [lroll(jnp.minimum(u[t], 0.0) * a[t], 8) for t in range(3)]
            fresh = []
            for t in range(size):
                value = lower[t] + jnp.maximum(u[t], 0.0) * a[t]
                value = value + jnp.where(lane >= 8, h[t], h[(t + 2) % 3])
                value = value + jnp.maximum(v[t], 0.0) * b[t]
                fresh.append(value + south[t])
            if step < NSUB:
                stages[step][row] = fresh
            else:
                for t in range(2):
                    out[t, pl.ds(base + row, 8, stride=16), :] = fresh[t]


def factor(k_in, f_v, r_v):
    lane = iota(1)
    low = lane < 64

    def block(m):
        return k_in[pl.ds(pl.multiple_of(8 * slot_of(m), 8), 8), :]

    a = jnp.where(low, 1.0, 1.0 + block(31))
    b = jnp.ones((8, 128), F32)

    def four(i, carry):
        a, b = carry
        for n in range(4):
            m = 4 * i + n
            here, there = block(m), block(31 - m)
            beyond = block(jnp.maximum(30 - m, 0))
            for l in range(2):
                if l == 0:
                    kappa = jnp.where(low, here, lroll(there, 64))
                else:
                    kappa = jnp.where(low, lroll(here, 64), beyond)
                last = a * b
                nexta, nextb = a + kappa * (a + b), a + kappa * b
                inv = b / nextb
                f_v[2 * m + l, :, :] = kappa * inv
                r_v[2 * m + l, :, :] = inv
                if n == 3 and l == 1:
                    p = a / b
                    other = lroll(p, 64)
                    det = 1.0 / (p * other + kappa * (p + other))

                    @pl.when(i == 3)
                    def _():
                        f_v[31, :, :] = kappa * det
                        r_v[31, :, :] = (other + kappa) * det

                a, b = nexta, nextb
        scale = 1.0 / b
        return (a * scale, jnp.ones((8, 128), F32))

    lax.fori_loop(0, 4, four, (a, b))


PLACES = [(h, t) for h in range(2) for t in range(2)]


def widen(f_v, r_v, f_w, r_w):
    column = iota(1) // 8

    def some(i, carry):
        for end in range(2):
            for n, (h, t) in enumerate(PLACES):
                index = column + (64 * end + 32 * h + 16 * t)
                for src, dst in ((f_v, f_w), (r_v, r_w)):
                    for j in range(8):
                        dst[8 * i + j, 4 * end + n, :, :] = lanes_of(src[8 * i + j, :, :], index)
        return carry

    lax.fori_loop(0, 4, some, 0)


def solve(x_v, f_w, r_w, out):
    spots = [(end, h, t) for end in range(2) for h, t in PLACES]

    def rows(j, end, h):
        level = j if end == 0 else 63 - j
        return pl.ds(pl.multiple_of(16 * level + 8 * h, 8), 8)

    def forward(i, carry):
        total, before = carry
        for n in range(4):
            j = 4 * i + n
            total = [x_v[t, rows(j, end, h), :] + f * s for (end, h, t), f, s in zip(spots, before, total)]
            before = [f_w[j, n, :, :] for n in range(8)]
            for n, (end, h, t) in enumerate(spots):
                x_v[t, rows(j, end, h), :] = r_w[j, n, :, :] * total[n]
        return (total, before)

    zeros = [jnp.zeros((8, 128), F32) for _ in spots]
    total, before = lax.fori_loop(0, 8, forward, (zeros, zeros))
    above = [r_w[31, n, :, :] * total[n] + before[n] * total[(n + 4) % 8] for n in range(8)]

    def put(j, values):
        for n, (end, h, t) in enumerate(spots):
            out[rows(j, end, h), 128 * t : 128 * t + 128] = values[n]

    put(31, above)

    def one(j, above):
        above = [x_v[t, rows(j, end, h), :] + f_w[j, n, :, :] * above[n] for n, (end, h, t) in enumerate(spots)]
        put(j, above)
        return above

    for n in range(1, 8):
        above = one(31 - n, above)

    def chunk(c, above):
        for n in range(8):
            above = one(31 - 8 * c - n, above)
        return above

    lax.fori_loop(1, 4, chunk, above)


def pack_surface(x_v, sf_v, turn, out):
    lane = lax.broadcasted_iota(jnp.int32, (32, 128), 1)
    for t in range(2):
        cols = slice(128 * t, 128 * t + 128)
        value = sf_v[:, cols] * x_v[t, 0:16, :]
        block = jnp.concatenate([value, jnp.zeros((112, 128), F32)], axis=0)
        turn[cols, :] = block.T
    total = turn[pl.ds(0, 32, stride=TRAC), :]
    for t in range(1, TRAC):
        piece = pltpu.roll(turn[pl.ds(t, 32, stride=TRAC), :], 16 * t, 1)
        total = jnp.where(jnp.logical_and(lane >= 16 * t, lane < 16 * t + 16), piece, total)
    out[...] = total


def unpack_flux(value, turn, out):
    for t in range(TRAC):
        piece = value if t == 0 else pltpu.roll(value, 128 - 16 * t, 1)
        turn[pl.ds(t, 32, stride=TRAC), :] = piece
    for t in range(2):
        cols = slice(128 * t, 128 * t + 128)
        out[:, cols] = turn[cols, :].T[:16]


def kernel(
    x_hbm, u_hbm, v_hbm, k_hbm, sf_hbm, zt_hbm, out, flux_out,
    x_v, u_v, v_v, k_v, sf_v, zt_v,
    uv_out, uv_in, uv_n, uv_s, ek_out, ek_in, e_in, e_n, e_s, k_in, f_v, r_v, f_w, r_w, w_v,
    lon_out, lon_h, lon_n, lon_s, lat_out, lat_n, lat_s, turn, ring, out_v,
    uv0_in, uv0_n, uv0_s, e0_in, e0_n, e0_s, y_v, zt_p, part_out, part_in, part_own,
    in_sem, ek_ss, ek_rs, uv_ss, uv_rs, lat_ss, lat_rs, lon_ss, lon_rs,
    cor_ss, cor_rs, fwd_ss, fwd_rs, far_ss, near_ss, part_ss, part_rs, ring_rs, out_sem, first_ss, first_rs,
):
    a, me = lax.axis_index("lat"), lax.axis_index("lon")
    z, x = lax.rem(me, NZ), me // NZ
    mine = slot_of(me)
    early = z < HALF
    has_n, has_s = a < NLA - 1, a > 0
    east = lax.rem(me + 1, NLO)
    west = lax.rem(me + NLO - 1, NLO)

    def tiled(ref, t):
        return ref.at[:, 128 * t : 128 * t + 128]

    pairs = ((u_hbm, u_v), (v_hbm, v_v), (k_hbm, k_v), (tiled(x_hbm, 0), x_v.at[0]), (tiled(x_hbm, 1), x_v.at[1]), (sf_hbm, sf_v), (zt_hbm, zt_v))
    loads = [pltpu.make_async_copy(src, dst, in_sem.at[i]) for i, (src, dst) in enumerate(pairs)]
    for load in loads:
        load.start()

    def each(count, action):
        def body(i, carry):
            action(i)
            return carry

        lax.fori_loop(0, count, body, 0)

    barrier = pltpu.get_barrier_semaphore()

    def nth(j):
        return lax.rem(j, 2) * NZ + j // 2

    def greet(lon):
        @pl.when(lon != me)
        def _():
            pl.semaphore_signal(barrier, inc=1, device_id=(a, lon), device_id_type=MESH)

    each(NLO // 2, lambda j: greet(nth(NLO // 2 + j)))

    each(NLO // 2, lambda j: greet(nth(j)))

    @pl.when(has_n)
    def _():
        pl.semaphore_signal(barrier, inc=1, device_id=(a + 1, me), device_id_type=MESH)

    @pl.when(has_s)
    def _():
        pl.semaphore_signal(barrier, inc=1, device_id=(a - 1, me), device_id_type=MESH)

    for load in loads[:3]:
        load.wait()
    pack_slabs(u_v, v_v, k_v, uv_out, ek_out, a == NLA - 1)
    loads[3].wait()
    loads[4].wait()
    pack_halos(x_v, lon_out, lat_out)

    uv_in[rows16(mine), :] = uv_out[rows16(mine), :]
    ek_in[mine] = ek_out[mine]

    @pl.when(jnp.logical_not(has_n))
    def _():
        for ref in (lat_n, lon_n, uv_n, e_n, uv0_n, e0_n):
            ref[...] = jnp.zeros_like(ref)

    @pl.when(jnp.logical_not(has_s))
    def _():
        for ref in (lat_s, lon_s, uv_s, e_s, uv0_s, e0_s):
            ref[...] = jnp.zeros_like(ref)

    for ref in (uv0_in, uv0_n, uv0_s):
        ref[16:64, :] = jnp.zeros((48, 128), F32)
    for ref in (e0_in, e0_n, e0_s):
        ref[8:32, :] = jnp.zeros((24, 128), F32)

    neighbours = jnp.where(has_n, 1, 0) + jnp.where(has_s, 1, 0)
    pl.semaphore_wait(barrier, NLO - 1 + neighbours)

    def remote(src, dst, ss, rs, device):
        return pltpu.make_async_remote_copy(
            src_ref=src, dst_ref=dst, send_sem=ss, recv_sem=rs, device_id=device, device_id_type=MESH
        )

    def send_ek(lon):
        s = slot_of(lon)
        return remote(ek_out.at[s], ek_in.at[mine], ek_ss.at[s], ek_rs.at[mine], (a, lon))

    def send_uv(lon):
        s = slot_of(lon)
        return remote(uv_out.at[rows16(s)], uv_in.at[rows16(mine)], uv_ss.at[s], uv_rs.at[mine], (a, lon))

    def recv_ek(slot):
        return remote(ek_out.at[slot], ek_in.at[slot], ek_ss.at[slot], ek_rs.at[slot], (a, lon_of(slot)))

    def recv_uv(slot):
        rows = rows16(slot)
        return remote(uv_out.at[rows], uv_in.at[rows], uv_ss.at[slot], uv_rs.at[slot], (a, lon_of(slot)))

    def span(c):
        return pl.ds(c * PER, PER)

    def lat_north(c):
        return remote(lat_out.at[1, span(c)], lat_s.at[span(c)], lat_ss.at[1, c], lat_rs.at[1, c], (a + 1, me))

    def lat_south(c):
        return remote(lat_out.at[0, span(c)], lat_n.at[span(c)], lat_ss.at[0, c], lat_rs.at[0, c], (a - 1, me))

    def lon_west(c):
        return remote(lon_out.at[0, :, span(c)], lon_h.at[0, :, span(c)], lon_ss.at[0, c], lon_rs.at[0, c], (a, west))

    def lon_east(c):
        return remote(lon_out.at[1, :, span(c)], lon_h.at[1, :, span(c)], lon_ss.at[1, c], lon_rs.at[1, c], (a, east))

    def cor_north(side, c):
        ref, dst = lon_h.at[side, 3, span(c)], lon_s.at[side, span(c)]
        return remote(ref, dst, cor_ss.at[1, side, c], cor_rs.at[1, side, c], (a + 1, me))

    def cor_south(side, c):
        ref, dst = lon_h.at[side, 0, span(c)], lon_n.at[side, span(c)]
        return remote(ref, dst, cor_ss.at[0, side, c], cor_rs.at[0, side, c], (a - 1, me))

    def uv_rows(group):
        return pl.ds(pl.multiple_of(64 * group, 64), 64)

    def e_rows(group):
        return pl.ds(pl.multiple_of(32 * group, 32), 32)

    def fwd_north(group):
        r, e = uv_rows(group), e_rows(group)
        return (
            remote(uv_in.at[r], uv_s.at[r], fwd_ss.at[1, 0, group], fwd_rs.at[1, 0, group], (a + 1, me)),
            remote(e_in.at[e], e_s.at[e], fwd_ss.at[1, 1, group], fwd_rs.at[1, 1, group], (a + 1, me)),
        )

    def fwd_south(group):
        r, e = uv_rows(group), e_rows(group)
        return (
            remote(uv_in.at[r], uv_n.at[r], fwd_ss.at[0, 0, group], fwd_rs.at[0, 0, group], (a - 1, me)),
            remote(e_in.at[e], e_n.at[e], fwd_ss.at[0, 1, group], fwd_rs.at[0, 1, group], (a - 1, me)),
        )

    def spread_blocks(order, first, count):
        def one(i):
            lon = lax.rem(first + i, 2) * NZ + order(first + i)

            @pl.when(lon != me)
            def _():
                send_ek(lon).start()
                send_uv(lon).start()

        each(count, one)

    def send_halos(first, count):
        def one(i):
            lon_east(first + i).start()
            lon_west(first + i).start()

            @pl.when(has_n)
            def _():
                lat_north(first + i).start()

            @pl.when(has_s)
            def _():
                lat_south(first + i).start()

        each(count, one)

    def along_z(j):
        return j // 2

    send_halos(0, 1)

    @pl.when(me == 0)
    def _():
        spread_blocks(lambda j: jnp.where(lax.rem(j // 2, 2) == 0, NZ - 1 - j // 4, j // 4), 0, NLO)

    @pl.when(me != 0)
    def _():
        spread_blocks(along_z, 0, NLO // 4)

    send_halos(1, CH - 1)

    @pl.when(me != 0)
    def _():
        spread_blocks(along_z, NLO // 4, NLO - NLO // 4)

    over = (1 - x) * NZ + z

    def zt_over():
        cols = pl.ds(pl.multiple_of((1 - x) * 512, 512), 512)
        return remote(zt_v.at[:, cols], zt_p, part_ss.at[0], part_rs.at[0], (a, over))

    loads[5].wait()
    loads[6].wait()
    zt_over().start()

    def corners(c):
        lon_west(c).wait_recv()
        lon_east(c).wait_recv()

        @pl.when(has_n)
        def _():
            cor_north(0, c).start()
            cor_north(1, c).start()

        @pl.when(has_s)
        def _():
            cor_south(0, c).start()
            cor_south(1, c).start()

    def halos_here(c):
        @pl.when(has_n)
        def _():
            lat_south(c).wait_recv()
            cor_south(0, c).wait_recv()
            cor_south(1, c).wait_recv()

        @pl.when(has_s)
        def _():
            lat_north(c).wait_recv()
            cor_north(0, c).wait_recv()
            cor_north(1, c).wait_recv()

    def first_north():
        return (
            remote(uv0_in.at[0:16], uv0_s.at[0:16], first_ss.at[1, 0], first_rs.at[1, 0], (a + 1, me)),
            remote(e0_in.at[0:8], e0_s.at[0:8], first_ss.at[1, 1], first_rs.at[1, 1], (a + 1, me)),
        )

    def first_south():
        return (
            remote(uv0_in.at[0:16], uv0_n.at[0:16], first_ss.at[0, 0], first_rs.at[0, 0], (a - 1, me)),
            remote(e0_in.at[0:8], e0_n.at[0:8], first_ss.at[0, 1], first_rs.at[0, 1], (a - 1, me)),
        )

    corners(0)

    @pl.when(me != 0)
    def _():
        recv_ek(0).wait_recv()
        recv_uv(0).wait_recv()

    uv0_in[0:16, :] = uv_in[0:16, :]
    e0_in[0:8, :] = jnp.concatenate([ek_in[0, 0, :, :], ek_in[0, 0, :, :]], axis=0)

    @pl.when(has_n)
    def _():
        for copy in first_north():
            copy.start()

    @pl.when(has_s)
    def _():
        for copy in first_south():
            copy.start()


    block = z // 4
    step = jnp.where(lax.rem(z, 4) < 2, 3, 1)

    def nth_group(i):
        k = i // 2
        shift = jnp.where(k == 0, 0, jnp.where(k == 1, step, jnp.where(k == 2, 4 - step, 2)))
        return 2 * lax.rem(block + shift, 4) + lax.rem(x + i, 2)

    def pass_on(group):
        def one(i):
            slot = 4 * group + i

            @pl.when(jnp.logical_and(slot != mine, slot != 0))
            def _():
                recv_ek(slot).wait_recv()
                recv_uv(slot).wait_recv()

            rims = ek_in[slot, 0, :, :]
            at = pl.multiple_of(8 * slot, 8)
            e_in[pl.ds(at, 8), :] = jnp.concatenate([rims, rims], axis=0)
            k_in[pl.ds(at, 8), :] = jnp.concatenate([ek_in[slot, 1, :, :], ek_in[slot, 2, :, :]], axis=0)

        each(4, one)

        @pl.when(has_n)
        def _():
            for copy in fwd_north(group):
                copy.start()

        @pl.when(has_s)
        def _():
            for copy in fwd_south(group):
                copy.start()


    def place(d):
        return lax.rem(z + d, NZ)

    place_in = lax.rem(z, 4)
    beyond = 4 * lax.rem(z // 4 + 2, 4)
    sent_beyond, from_beyond = beyond + lax.rem(place_in + 3, 4), beyond + lax.rem(place_in + 1, 4)
    far_to = (place(4), place(12), sent_beyond)
    held = (z, place(4), place(12), from_beyond)

    def ring_send(block, device, sem):
        return remote(ring.at[block], ring.at[block], sem, ring_rs.at[block], (a, device))

    def ring_far(i):
        return ring_send(me, x * NZ + far_to[i], far_ss.at[i])

    def ring_near(k, i):
        block = x * NZ + held[k]
        return ring_send(block, x * NZ + 4 * (z // 4) + lax.rem(z + 1 + i, 4), near_ss.at[k, i])

    def ring_recv(block):
        return ring_send(block, over, part_ss.at[0])

    def part_over():
        return remote(part_out, part_in, part_ss.at[1], part_rs.at[1], (a, over))

    def ring_start():
        pack_surface(y_v, sf_v, turn, ring.at[me])
        for i in range(3):
            ring_far(i).start()
        for i in range(3):
            ring_near(0, i).start()

    def ring_middle():
        for k in range(1, 4):
            ring_recv(x * NZ + held[k]).wait_recv()
            for i in range(3):
                ring_near(k, i).start()

    def ring_end():
        for d in range(1, NZ):
            if d not in (4, 12):

                @pl.when(place(d) != from_beyond)
                def _():
                    ring_recv(x * NZ + place(d)).wait_recv()

        gathered = ring[pl.ds(x * NZ, NZ)].reshape(NZ * 32, 128)
        zt_over().wait_recv()
        part_out[...] = jnp.dot(zt_p[...], gathered, precision=lax.Precision.HIGHEST, preferred_element_type=F32)
        part_over().start()
        own = zt_v[:, pl.ds(pl.multiple_of(x * 512, 512), 512)]
        part_own[...] = jnp.dot(own, gathered, precision=lax.Precision.HIGHEST, preferred_element_type=F32)

    halos_here(0)

    @pl.when(has_n)
    def _():
        for copy in first_south():
            copy.wait_recv()

    @pl.when(has_s)
    def _():
        for copy in first_north():
            copy.wait_recv()

    transport(0, x_v, uv0_in, uv0_n, uv0_s, e0_in, e0_n, e0_s, lon_h, lon_n, lon_s, lat_n, lat_s, w_v, y_v, 0)
    ring_start()
    each(CH - 1, lambda c: corners(c + 1))
    ring_middle()
    each(LOOK, lambda i: pass_on(nth_group(i)))

    def turn_of(i):
        group = nth_group(i)

        @pl.when(i + LOOK < NG)
        def _():
            pass_on(nth_group(i + LOOK))

        @pl.when(jnp.logical_and(lax.rem(i, PER) == 0, group // PER > 0))
        def _():
            halos_here(group // PER)

        @pl.when(has_n)
        def _():
            for copy in fwd_south(group):
                copy.wait_recv()

        @pl.when(has_s)
        def _():
            for copy in fwd_north(group):
                copy.wait_recv()

        transport(
            group, x_v, uv_in, uv_n, uv_s, e_in, e_n, e_s, lon_h, lon_n, lon_s, lat_n, lat_s, w_v, x_v, level_base(group)
        )

        @pl.when(i == 1)
        def _():
            ring_end()

        @pl.when(i == NG - LOOK)
        def _():
            factor(k_in, f_v, r_v)
            widen(f_v, r_v, f_w, r_w)

    each(NG, turn_of)

    def store(c):
        rows = pl.ds(256 * c, 256)
        return pltpu.make_async_copy(out_v.at[rows], out.at[rows], out_sem.at[c])

    solve(x_v, f_w, r_w, out_v)
    for c in range(4):
        store(c).start()

    part_over().wait_recv()
    unpack_flux(part_own[...] + part_in[...], turn, flux_out)

    def sent(lon):
        @pl.when(lon != me)
        def _():
            send_ek(lon).wait_send()
            send_uv(lon).wait_send()

    each(NLO, sent)
    for c in range(4):
        store(c).wait()

    def sent_group(group):
        @pl.when(has_n)
        def _():
            for copy in fwd_north(group):
                copy.wait_send()

        @pl.when(has_s)
        def _():
            for copy in fwd_south(group):
                copy.wait_send()

    each(NG, sent_group)

    @pl.when(has_n)
    def _():
        for copy in first_north():
            copy.wait_send()

    @pl.when(has_s)
    def _():
        for copy in first_south():
            copy.wait_send()

    def sent_chunk(c):
        lon_east(c).wait_send()
        lon_west(c).wait_send()

        @pl.when(has_n)
        def _():
            lat_north(c).wait_send()
            cor_north(0, c).wait_send()
            cor_north(1, c).wait_send()

        @pl.when(has_s)
        def _():
            lat_south(c).wait_send()
            cor_south(0, c).wait_send()
            cor_south(1, c).wait_send()

    each(CH, sent_chunk)
    for i in range(3):
        ring_far(i).wait_send()
        for k in range(4):
            ring_near(k, i).wait_send()
    zt_over().wait_send()
    part_over().wait_send()


def on_device(adjoint_in, u_courant, v_courant, diffusivity, surface_factor, zonal_sqrt):
    def vmem(*shape):
        return pltpu.VMEM(shape, F32)

    def dma(*shape):
        return pltpu.SemaphoreType.DMA(shape)

    solved, flux = pl.pallas_call(
        kernel,
        name="adjoint_hour",
        out_shape=(
            jax.ShapeDtypeStruct((1024, 256), F32),
            jax.ShapeDtypeStruct(surface_factor.shape, F32),
        ),
        in_specs=[pl.BlockSpec(memory_space=pltpu.HBM)] * 6,
        out_specs=(pl.BlockSpec(memory_space=pl.ANY), pl.BlockSpec(memory_space=pltpu.VMEM)),
        scratch_shapes=[
            vmem(2, 1024, 128), vmem(2, 16, 1024), vmem(2, 16, 1024), vmem(2, 16, 1024),
            vmem(16, 256), vmem(32, 1024),
            vmem(512, 128), vmem(512, 128), vmem(512, 128), vmem(512, 128),
            vmem(32, 3, 4, 128), vmem(32, 3, 4, 128), vmem(256, 128), vmem(256, 128), vmem(256, 128), vmem(256, 128),
            vmem(32, 8, 128), vmem(32, 8, 128), vmem(32, 8, 8, 128), vmem(32, 8, 8, 128), vmem(2, 24, 3, 8, 128),
            vmem(2, 4, 8, 8, 128), vmem(2, 4, 8, 8, 128), vmem(2, 8, 8, 128), vmem(2, 8, 8, 128),
            vmem(2, 8, 4, 8, 256), vmem(8, 4, 8, 256), vmem(8, 4, 8, 256), vmem(256, 128), vmem(32, 32, 128), vmem(1024, 256),
            vmem(64, 128), vmem(64, 128), vmem(64, 128), vmem(32, 128), vmem(32, 128), vmem(32, 128), vmem(2, 128, 128),
            vmem(32, 512), vmem(32, 128), vmem(32, 128), vmem(32, 128),
            dma(7), dma(32), dma(32), dma(32), dma(32), dma(2, CH), dma(2, CH), dma(2, CH), dma(2, CH),
            dma(2, 2, CH), dma(2, 2, CH), dma(2, 2, NG), dma(2, 2, NG), dma(3), dma(4, 3), dma(2), dma(2), dma(32), dma(4), dma(2, 2), dma(2, 2),
        ],
        compiler_params=pltpu.CompilerParams(
            collective_id=0, has_side_effects=True, vmem_limit_bytes=56 * 2**20
        ),
        cost_estimate=pl.CostEstimate(flops=60_000_000, bytes_accessed=3_000_000, transcendentals=0),
    )(adjoint_in.reshape(1024, 256), u_courant, v_courant, diffusivity, surface_factor, zonal_sqrt.T)
    return solved.reshape(adjoint_in.shape), flux


def solution(mesh):
    placed = (
        P(None, "lat", "lon"),
        P("lon", "lat", None),
        P("lon", "lat", None),
        P("lon", "lat", None),
        P("lat", "lon"),
        P(None, "lon"),
    )
    return jax.shard_map(
        on_device,
        mesh=mesh,
        in_specs=placed,
        out_specs=(P(None, "lat", "lon"), P("lat", "lon")),
        check_vma=False,
    )
```
